256 devices in a mesh: row: 16 (over z, core), col: 16 (over x, y).
Axes of the slice: x: 4, y: 4, z: 8, core: 2. Of those that a mesh axis runs over, the one named last changes fastest.
Arguments:
- inputs: bfloat16 [32, 1048576], P(None, ('row', 'col')), may hold values from -6 to 6
- morton_order: int32 [1048576], P(('row', 'col')), may hold values from 0 to 4095, as said below
- basis: bfloat16 [4096, 64, 256], P(('row', 'col')), may hold values from -0.375 to 0.375
- leaf_up: float32 [16, 64, 64], replicated, may hold values from -0.1875 to 0.1875
- up_transfer: float32 [16, 30, 64, 64], P('row'), may hold values from -0.5 to 0.5
- couple_leaf: bfloat16 [4096, 4, 64, 64], P(('row', 'col')), may hold values from -0.375 to 0.375
- leaf_lists: int32 [4096, 4], P(('row', 'col')), may hold values from 0 to 4095, as said below
- couple_row: bfloat16 [16, 3, 64, 64], P('row'), may hold values from -7 to 7
- row_lists: int32 [16, 3], P('row'), may hold values from 0 to 15, as said below
- near_blocks: bfloat16 [4096, 4, 256, 256], P(('row', 'col')), may hold values from -0.1875 to 0.1875
- near_offsets: int32 [4096, 4], P(('row', 'col')), may hold values from -4 to 4, as said below
Outputs:
- product: bfloat16 [32, 1048576], P(None, ('row', 'col'))
The draws below stay inside these ranges and needn't reach their ends.
Inputs may be any that keep to these rules, and one draw needn't show every extreme that they name: `morton_order`: each device block of 4096 entries is a permutation of 0 .. 4095. `near_offsets`: the 4 offsets of a leaf are distinct. `leaf_lists`: source k of a leaf in device block (r, c) is a leaf of device block (r, (c + o_k) mod 16) of the same outer node, with o_0 = 15, o_1 = 8 and o_k = k - 1 for k >= 2, more than 4 leaves from the target in that node's cyclic leaf order. `row_lists`: the 3 sources of an outer node are distinct and differ from it.
All inputs are finite; a program needn't handle non-finite values.
Results may differ from the reference program's by a relative error of at most 0.0055.
Values may be sent and summed in bfloat16 or wider, within the bound.
No kernel may reach another device: no remote copies, remote signals or barrier semaphores. Data moves between devices by JAX's collectives and lax.ppermute only.
A program may use at most 64 MiB of HBM per device.

```python
import jax
import jax.numpy as jnp
from jax import lax

PTS = 256
RANK = 64
NRHS = 32
LEAF_DEV = 16
REACH = 4
NEAR = 4
K0 = 4
K1 = 3
PTS_DEV = 4096
ROW_LEAVES = 256
LEAVES = 4096
POINTS = 1048576
COL_LEVELS = 4
N_ROW = 16
N_COL = 16


def draw_morton_order(key, part):
    key = jax.random.fold_in(key, 11)
    keys = jax.random.split(key, N_ROW * N_COL)

    def one_block(block_key):
        return jax.random.permutation(block_key, PTS_DEV)
    return jax.vmap(one_block)(keys).reshape(-1).astype(jnp.int32)


def draw_near_offsets(key, part):
    key = jax.random.fold_in(key, 23)
    keys = jax.random.split(key, LEAVES)

    def one_leaf(leaf_key):
        return jax.random.permutation(leaf_key, 2 * REACH + 1)[:NEAR]
    return (jax.vmap(one_leaf)(keys) - REACH).astype(jnp.int32)


def draw_leaf_lists(key, part):
    key = jax.random.fold_in(key, 37)
    leaf_ids = jnp.arange(LEAVES, dtype=jnp.int32)[:, None]
    slots = jnp.arange(K0, dtype=jnp.int32)[None, :]
    row_base = leaf_ids // ROW_LEAVES * ROW_LEAVES
    within = leaf_ids % ROW_LEAVES
    block_col = within // LEAF_DEV
    position = within % LEAF_DEV
    slot_offset = jnp.where(slots == 0, N_COL - 1, jnp.where(slots == 1, N_COL // 2, slots - 1)).astype(jnp.int32)
    peer = (block_col + slot_offset) % N_COL
    lowest = jnp.where(slot_offset == 1, jnp.maximum(position + REACH + 1 - LEAF_DEV, 0), 0).astype(jnp.int32)
    highest = jnp.where(slots == 0, jnp.minimum(position + LEAF_DEV - REACH, LEAF_DEV), LEAF_DEV).astype(jnp.int32)
    lowest = jnp.broadcast_to(lowest, (LEAVES, K0))
    highest = jnp.broadcast_to(highest, (LEAVES, K0))
    picked = jax.random.randint(key, (LEAVES, K0), lowest, highest, dtype=jnp.int32)
    return (row_base + peer * LEAF_DEV + picked).astype(jnp.int32)


def draw_row_lists(key, part):
    key = jax.random.fold_in(key, 53)
    keys = jax.random.split(key, N_ROW)

    def one_node(node_key):
        return jax.random.permutation(node_key, N_ROW - 1)[:K1]
    chosen = jax.vmap(one_node)(keys).astype(jnp.int32)
    node_ids = jnp.arange(N_ROW, dtype=jnp.int32)[:, None]
    return (chosen + (chosen >= node_ids).astype(jnp.int32)).astype(jnp.int32)


def block_scale(own_key, shape, cuts, low, high):
    loudness, own = 1.0, jax.random.fold_in(own_key, 6)
    for dim, shards_of in cuts:
        steps = jnp.exp(jax.random.uniform(jax.random.fold_in(own, dim), (shards_of,), jnp.float32, low / len(cuts), high / len(cuts)))
        loudness = loudness * jnp.repeat(steps, shape[dim] // shards_of).reshape([-1 if axis == dim else 1 for axis in range(len(shape))])
    return loudness


def noise(own_key, dims, width, most, shards=(), kind=jnp.bfloat16):
    result = jax.random.normal(own_key, dims, jnp.float32) * width
    if len(shards) > 0:
        result = block_scale(own_key, dims, shards, -0.22, 0.18) * result
    return jnp.clip(result, min=-most, max=most).astype(kind)


def setup_inputs(seed: int = 0) -> dict:
    splits = jax.random.split(jax.random.key(seed), 12)
    inputs = noise(splits[0], (NRHS, POINTS), 1.0, 6.0, ((1, 256),))
    morton_order = draw_morton_order(jax.random.fold_in(splits[11], 71), 0)
    basis = noise(splits[2], (LEAVES, RANK, PTS), PTS ** -0.5, 0.375, ((0, 256),))
    leaf_up = noise(splits[3], (LEAF_DEV, RANK, RANK), (RANK * LEAF_DEV) ** -0.5, 0.1875, (), jnp.float32)
    up_transfer = noise(splits[4], (N_ROW, 2 * N_COL - 2, RANK, RANK), (2 * RANK) ** -0.5, 0.5, ((0, 16),), jnp.float32)
    couple_leaf = noise(splits[5], (LEAVES, K0, RANK, RANK), (RANK * K0) ** -0.5, 0.375, ((0, 256),))
    leaf_lists = draw_leaf_lists(jax.random.fold_in(splits[11], 71), 0)
    couple_row = noise(splits[7], (N_ROW, K1, RANK, RANK), ((N_COL * LEAF_DEV) ** 0.5 * (RANK * K1) ** -0.5), 7.0, ((0, 16),))
    row_lists = draw_row_lists(jax.random.fold_in(splits[11], 71), 0)
    near_blocks = noise(splits[9], (LEAVES, NEAR, PTS, PTS), (PTS * NEAR) ** -0.5, 0.1875, ((0, 256),))
    near_offsets = draw_near_offsets(jax.random.fold_in(splits[11], 71), 0)
    return dict(inputs=inputs, morton_order=morton_order, basis=basis, leaf_up=leaf_up, up_transfer=up_transfer, couple_leaf=couple_leaf, leaf_lists=leaf_lists, couple_row=couple_row, row_lists=row_lists, near_blocks=near_blocks, near_offsets=near_offsets)


def reference(inputs, morton_order, basis, leaf_up, up_transfer, couple_leaf, leaf_lists, couple_row, row_lists, near_blocks, near_offsets):
    highest = lax.Precision.HIGHEST
    node_count = N_ROW * N_COL
    blocks = inputs.reshape(NRHS, node_count, PTS_DEV)
    local_order = morton_order.reshape(node_count, PTS_DEV)
    ordered = jnp.take_along_axis(blocks, local_order[None, :, :], axis=2)
    leaves = ordered.reshape(NRHS, LEAVES, PTS)
    multipoles = jnp.einsum("nlp,lrp->lnr", leaves.astype(jnp.float32), basis.astype(jnp.float32)).astype(jnp.bfloat16)
    device_poles = jnp.einsum("dlns,lst->dnt", multipoles.reshape(node_count, LEAF_DEV, NRHS, RANK).astype(jnp.float32), leaf_up, precision=highest)
    climbing = device_poles.reshape(N_ROW, N_COL, NRHS, RANK)
    for height in range(COL_LEVELS):
        node_span = N_COL // 2 ** height
        heap_first = 2 * N_COL - 2 * node_span
        lifted = jnp.einsum("rcns,rcst->rcnt", climbing, up_transfer[:, heap_first:heap_first + node_span], precision=highest)
        climbing = lifted.reshape(N_ROW, node_span // 2, 2, NRHS, RANK).sum(axis=2)
    row_wire = climbing[:, 0].astype(jnp.bfloat16)
    row_picked = row_wire[row_lists]
    row_local = jnp.einsum("rkns,rkst->rnt", row_picked.astype(jnp.float32), couple_row.astype(jnp.float32))
    downward = row_local[:, None]
    for height in reversed(range(COL_LEVELS)):
        node_span = N_COL // 2 ** height
        heap_first = 2 * N_COL - 2 * node_span
        downward = jnp.repeat(downward, 2, axis=1)
        downward = jnp.einsum("rcnt,rcst->rcns", downward, up_transfer[:, heap_first:heap_first + node_span], precision=highest)
    downward = downward.reshape(node_count, NRHS, RANK)
    leaf_picked = multipoles[leaf_lists]
    coupled = jnp.einsum("lkns,lkst->lnt", leaf_picked.astype(jnp.float32), couple_leaf.astype(jnp.float32))
    pushed = jnp.einsum("dns,lts->dlnt", downward, leaf_up, precision=highest).reshape(LEAVES, NRHS, RANK)
    leaf_local = (coupled + pushed).astype(jnp.bfloat16)
    far_part = jnp.einsum("lnr,lrp->nlp", leaf_local.astype(jnp.float32), basis.astype(jnp.float32))
    padded = jnp.pad(leaves, ((0, 0), (REACH, REACH), (0, 0)))
    source_pos = (jnp.arange(LEAVES, dtype=jnp.int32)[:, None] + REACH + near_offsets).reshape(node_count, LEAF_DEV, NEAR)

    def near_device(paired):
        device_blocks, positions = paired
        sources = padded[:, positions].astype(jnp.float32)
        return jnp.einsum("nlks,lkst->nlt", sources, device_blocks.astype(jnp.float32))

    near_part = lax.map(near_device, (near_blocks.reshape(node_count, LEAF_DEV, NEAR, PTS, PTS), source_pos))
    near_part = jnp.transpose(near_part, (1, 0, 2, 3)).reshape(NRHS, LEAVES, PTS)
    summed = (near_part + far_part).astype(jnp.bfloat16).reshape(NRHS, node_count, PTS_DEV)
    row_ids = jnp.arange(node_count, dtype=jnp.int32)[:, None]
    scattered = jnp.zeros_like(summed).at[:, row_ids, local_order].set(summed)
    return scattered.reshape(NRHS, POINTS)
```

```python
import jax
import jax.numpy as jnp
from jax import lax
from jax.experimental import pallas as pl
from jax.experimental.pallas import tpu as pltpu
from jax.sharding import PartitionSpec as P

REACH = 4
BF = jnp.bfloat16
F32 = jnp.float32
HIGHEST = lax.Precision.HIGHEST
VMEM = pl.BlockSpec(memory_space=pltpu.VMEM)
SMEM = pl.BlockSpec(memory_space=pltpu.SMEM)
ANY = pl.BlockSpec(memory_space=pl.ANY)
LANES = 128
GROUP = 2
AHEAD = 8


def in_hbm(value):
    return pltpu.with_memory_space_constraint(value, pltpu.HBM)


def mm(a, b):
    return jnp.dot(a, b, preferred_element_type=F32)


def mm_t(a, b):
    return lax.dot_general(a, b, (((1,), (1,)), ((), ())), preferred_element_type=F32)


def halves(value):
    high = value.astype(BF)
    return high, (value - high.astype(F32)).astype(BF)


def one_hot(low, size):
    rows = lax.broadcasted_iota(jnp.int32, (size, low.shape[1]), 0).astype(BF)
    wanted = jnp.broadcast_to(low.astype(BF), rows.shape)
    return jnp.where(rows == wanted, jnp.ones_like(rows), jnp.zeros_like(rows))


def up_kernel(
    place, x_hbm, order_hbm, basis_hbm, leaf_up_hbm, up, lifted, first_out, second_out, poles, ordered, chain,
    x, order, basis, leaf_up, steps, sems,
):
    leaf_count, rank, points = basis.shape
    rhs = x.shape[0]
    depth = steps.shape[0]
    half = leaf_count // 2
    edge = 2 * REACH
    col, cols = place[0], lifted.shape[0]
    first = [
        pltpu.make_async_copy(order_hbm, order, sems.at[0]),
        pltpu.make_async_copy(x_hbm, x, sems.at[1]),
    ]
    for h in range(depth):
        node = 2 * cols - 2 * (cols >> h) + (col >> h)
        first.append(pltpu.make_async_copy(up.at[0, node], steps.at[h], sems.at[4 + h]))
    second = [pltpu.make_async_copy(basis_hbm, basis, sems.at[2])]
    third = [pltpu.make_async_copy(leaf_up_hbm, leaf_up, sems.at[3])]
    for copy in first + second + third:
        copy.start()
    for copy in first:
        copy.wait()
    whole = steps[0]
    for h in range(1, depth):
        whole = jnp.dot(whole, steps[h], precision=HIGHEST, preferred_element_type=F32)
    chain[...] = whole
    slabs = jnp.concatenate(
        [x[:, a * points : (a + 1) * points] for a in range(leaf_count)], axis=0
    )
    leaves = []
    for i in range(leaf_count):
        where = order[:, i * points : (i + 1) * points]
        low = where & (points - 1)
        high = jnp.broadcast_to(where // points, (8, points))
        picked = mm(slabs, one_hot(low, points)).reshape(leaf_count, rhs // 8, 8, points)
        total = picked[0]
        for a in range(1, leaf_count):
            total = jnp.where((high == a)[None], picked[a], total)
        leaf = total.reshape(rhs, points).astype(BF)
        ordered[2 * i] = leaf[:, :LANES]
        ordered[2 * i + 1] = leaf[:, LANES:]
        leaves.append(leaf)
    for copy in second:
        copy.wait()
    moments = [mm_t(leaves[i], basis[i]).astype(BF) for i in range(leaf_count)]
    pairs = [jnp.concatenate(moments[i : i + 2], axis=1) for i in range(0, leaf_count, 2)]
    for q in range(half):
        poles[q] = pairs[q]
        first_out[edge + q] = pairs[q]
        second_out[edge + q] = pairs[q]
    for copy in third:
        copy.wait()
    up_high, up_low = halves(leaf_up[...].reshape(leaf_count * rank, rank))
    every = jnp.concatenate(pairs, axis=1)
    top = mm(every, up_high) + mm(every, up_low)
    top = jnp.dot(top, whole, precision=HIGHEST, preferred_element_type=F32)
    packed = jnp.concatenate([top[: rhs // 2], top[rhs // 2 :]], axis=1)
    for c in range(cols):
        lifted[c] = packed
    odd = (col & 1) == 1
    head, tail = ordered[:edge], ordered[2 * leaf_count - edge :]
    first_out[:edge] = jnp.where(odd, tail, head)
    second_out[:edge] = jnp.where(odd, head, tail)


def up_call(place, inputs, order, basis, leaf_up, up_transfer, cols):
    rhs = inputs.shape[0]
    leaf_count, rank, points = basis.shape
    depth = cols.bit_length() - 1
    shape = jax.ShapeDtypeStruct
    half = leaf_count // 2
    sent = shape((2 * REACH + half, rhs, LANES), BF)
    return pl.pallas_call(
        up_kernel,
        out_shape=(
            shape((cols, rhs // 2, LANES), F32),
            sent,
            sent,
            shape((half, rhs, LANES), BF),
            shape((2 * leaf_count, rhs, LANES), BF),
            shape((rank, rank), F32),
        ),
        in_specs=[SMEM] + [ANY] * 5,
        out_specs=(VMEM,) * 6,
        scratch_shapes=[
            pltpu.VMEM(inputs.shape, BF),
            pltpu.VMEM(order.shape, order.dtype),
            pltpu.VMEM(basis.shape, BF),
            pltpu.VMEM(leaf_up.shape, F32),
            pltpu.VMEM((depth, rank, rank), F32),
            pltpu.SemaphoreType.DMA((4 + depth,)),
        ],
        compiler_params=pltpu.CompilerParams(vmem_limit_bytes=24 << 20),
        cost_estimate=pl.CostEstimate(flops=1 << 32, bytes_accessed=3 << 20, transcendentals=0),
        name="up",
    )(place, in_hbm(inputs), in_hbm(order), in_hbm(basis), in_hbm(leaf_up), in_hbm(up_transfer))


def near_kernel(place, offsets, ordered, first, second, blocks_hbm, near, extended, blocks, sems):
    leaf_count, count, points, _ = blocks.shape
    col, row, rows, cols = place[0], place[1], place[2], place[3]
    edge = 2 * REACH
    group = leaf_count // sems.shape[0]
    fetched = [
        pltpu.make_async_copy(
            blocks_hbm.at[i : i + group], blocks.at[i : i + group], sems.at[i // group]
        )
        for i in range(0, leaf_count, group)
    ]
    for copy in fetched[:AHEAD]:
        copy.start()
    odd = (col & 1) == 1
    lowest = (col == 0) & (row == 0)
    highest = (col == cols - 1) & (row == rows - 1)
    before = jnp.where(odd, second[:edge], first[:edge])
    after = jnp.where(odd, first[:edge], second[:edge])
    extended[edge : edge + 2 * leaf_count] = ordered[...]
    extended[:edge] = jnp.where(lowest, jnp.zeros_like(before), before)
    extended[edge + 2 * leaf_count :] = jnp.where(highest, jnp.zeros_like(after), after)
    for i in range(leaf_count):
        if i % group == 0:
            fetched[i // group].wait()
            if i // group + AHEAD < len(fetched):
                fetched[i // group + AHEAD].start()
        parts = []
        for k in range(count):
            at = 2 * (i + REACH + offsets[k, i])
            parts += [extended[at], extended[at + 1]]
        near[i] = mm(jnp.concatenate(parts, axis=1), blocks[i].reshape(count * points, points))


def near_call(place, offsets, ordered, first, second, near_blocks):
    leaf_count, _, points, _ = near_blocks.shape
    rhs = ordered.shape[1]
    return pl.pallas_call(
        near_kernel,
        out_shape=jax.ShapeDtypeStruct((leaf_count, rhs, points), F32),
        in_specs=[SMEM, SMEM] + [VMEM] * 3 + [ANY],
        out_specs=VMEM,
        scratch_shapes=[
            pltpu.VMEM((2 * leaf_count + 4 * REACH, rhs, LANES), BF),
            pltpu.VMEM(near_blocks.shape, BF),
            pltpu.SemaphoreType.DMA((leaf_count // GROUP,)),
        ],
        compiler_params=pltpu.CompilerParams(vmem_limit_bytes=24 << 20),
        cost_estimate=pl.CostEstimate(flops=1 << 30, bytes_accessed=10 << 20, transcendentals=0),
        name="near",
    )(place, offsets, ordered, first, second, in_hbm(near_blocks))


def down_kernel(
    place, lists, row_lists, first, second, around, p1, p3, couple_hbm, rows, couple_row, chain, leaf_up,
    basis, near, order, out, poles, couple, spread, marks, sem,
):
    leaf_count, rank, points = basis.shape
    rhs = near.shape[1]
    slots = couple.shape[1]
    edge = 2 * REACH
    col, cols = place[0], place[3]
    fetched = pltpu.make_async_copy(couple_hbm, couple, sem)
    fetched.start()
    odd = (col & 1) == 1
    poles[0] = jnp.where(odd, second[edge:], first[edge:])
    poles[2] = jnp.where(odd, first[edge:], second[edge:])
    poles[1] = p1[...]
    poles[3] = p3[...]

    @pl.when(col == 0)
    def _():
        poles[0] = around[...]

    @pl.when(col == cols - 1)
    def _():
        poles[2] = around[...]

    for i in range(leaf_count):
        where = order[:, i * points : (i + 1) * points]
        marks[:, i * points : (i + 1) * points] = one_hot(where & (points - 1), points)
    joined = []
    for i in range(leaf_count):
        parts = []
        for k in range(slots):
            source = lists[k, i] & (leaf_count - 1)
            pair = poles[k, source // 2]
            parts.append(jnp.where((source & 1) == 1, pair[:, rank:], pair[:, :rank]))
        joined.append(jnp.concatenate(parts, axis=1))
    sources = []
    for k in range(couple_row.shape[1]):
        packed = rows[row_lists[0, k]]
        sources.append(jnp.concatenate([packed[:, :rank], packed[:, rank:]], axis=0))
    local_row = mm(
        jnp.concatenate(sources, axis=1), couple_row[0].reshape(len(sources) * rank, rank)
    )
    fetched.wait()
    sides = [mm(joined[i], couple[i].reshape(slots * rank, rank)) for i in range(leaf_count)]
    downward = lax.dot_general(
        local_row, chain[...], (((1,), (1,)), ((), ())), precision=HIGHEST, preferred_element_type=F32
    )
    down_high, down_low = halves(downward)
    up_high, up_low = halves(leaf_up[...].reshape(leaf_count * rank, rank))
    both = mm_t(jnp.concatenate([down_high, down_low], axis=0), up_high)
    pushed = both[:rhs] + both[rhs:] + mm_t(down_high, up_low)
    leaf_local = (jnp.concatenate(sides, axis=1) + pushed).astype(BF)
    fars = [mm(leaf_local[:, i * rank : (i + 1) * rank], basis[i]) for i in range(leaf_count)]
    for i in range(leaf_count):
        high = (order[:, i * points : (i + 1) * points] // points).astype(BF)
        high = jnp.broadcast_to(high, (rhs, points))
        summed = (near[i] + fars[i]).astype(BF)
        for a in range(leaf_count):
            spread[a * rhs : (a + 1) * rhs, i * points : (i + 1) * points] = jnp.where(
                high == a, summed, jnp.zeros_like(summed)
            )
    total = mm_t(spread[...], marks[...]).astype(BF)
    for a in range(leaf_count):
        out[:, a * points : (a + 1) * points] = total[a * rhs : (a + 1) * rhs]


def down_call(
    place, lists, row_lists, first, second, around, p1, p3, couple, row_poles, couple_row, chain, leaf_up,
    basis, near, order,
):
    leaf_count, rank, points = basis.shape
    rhs = near.shape[1]
    return pl.pallas_call(
        down_kernel,
        out_shape=jax.ShapeDtypeStruct((rhs, leaf_count * points), BF),
        in_specs=[SMEM] * 3 + [VMEM] * 5 + [ANY] + [VMEM] * 7,
        out_specs=VMEM,
        scratch_shapes=[
            pltpu.VMEM((couple.shape[1], *p1.shape), BF),
            pltpu.VMEM(couple.shape, BF),
            pltpu.VMEM((leaf_count * rhs, leaf_count * points), BF),
            pltpu.VMEM((points, leaf_count * points), BF),
            pltpu.SemaphoreType.DMA,
        ],
        compiler_params=pltpu.CompilerParams(vmem_limit_bytes=24 << 20),
        cost_estimate=pl.CostEstimate(flops=1 << 30, bytes_accessed=3 << 20, transcendentals=0),
        name="down",
    )(
        place, lists, row_lists, first, second, around, p1, p3, in_hbm(couple), row_poles, couple_row,
        chain, leaf_up, basis, near, order,
    )


def local(
    inputs,
    morton_order,
    basis,
    leaf_up,
    up_transfer,
    couple_leaf,
    leaf_lists,
    couple_row,
    row_lists,
    near_blocks,
    near_offsets,
):
    cols = lax.axis_size("col")
    rows = lax.axis_size("row")
    count = rows * cols
    place = jnp.stack([lax.axis_index("col"), lax.axis_index("row"), rows, cols]).astype(jnp.int32)
    order = morton_order.reshape(1, -1)
    lifted, first, second, poles, ordered, chain = up_call(
        place, inputs, order, basis, leaf_up, up_transfer, cols
    )
    everyone = lax.all_to_all(lifted, "col", 0, 0, tiled=True)

    def swap(value, start):
        pairs = [(b, (b + 1) % count) for b in range(start, count, 2)]
        return lax.ppermute(value, ("row", "col"), pairs + [(b, a) for a, b in pairs])

    def from_peer(value, away):
        return lax.ppermute(value, "col", [((c + away) % cols, c) for c in range(cols)])

    first = swap(first, 1)
    row_wire = everyone.sum(axis=0).astype(BF)
    row_wire = jnp.broadcast_to(row_wire[None], (rows,) + row_wire.shape)
    row_poles = lax.all_to_all(row_wire, "row", 0, 0, tiled=True)
    second = swap(second, 0)
    p1 = from_peer(poles, cols // 2)
    p3 = from_peer(poles, 2)
    turn = [(((r + 1) % rows) * cols, r * cols) for r in range(rows)]
    turn += [(r * cols + cols - 1, ((r + 1) % rows) * cols + cols - 1) for r in range(rows)]
    around = lax.ppermute(first[2 * REACH :], ("row", "col"), turn)
    near = near_call(place, near_offsets.T, ordered, first, second, near_blocks)
    return down_call(
        place, leaf_lists.T, row_lists, first, second, around, p1, p3, couple_leaf, row_poles, couple_row,
        chain, leaf_up, basis, near, order,
    )


def solution(mesh):
    return jax.shard_map(
        local,
        mesh=mesh,
        in_specs=(
            P(None, ("row", "col")),
            P(("row", "col")),
            P(("row", "col"), None, None),
            P(),
            P("row", None, None, None),
            P(("row", "col"), None, None, None),
            P(("row", "col"), None),
            P("row", None, None, None),
            P("row", None),
            P(("row", "col"), None, None, None),
            P(("row", "col"), None),
        ),
        out_specs=P(None, ("row", "col")),
        check_vma=False,
    )
```

```python
import jax
import jax.numpy as jnp
from jax import lax
from jax.experimental import pallas as pl
from jax.experimental.pallas import tpu as pltpu
from jax.sharding import PartitionSpec as P

REACH = 4
BF = jnp.bfloat16
F32 = jnp.float32
HIGHEST = lax.Precision.HIGHEST
VMEM = pl.BlockSpec(memory_space=pltpu.VMEM)
SMEM = pl.BlockSpec(memory_space=pltpu.SMEM)
ANY = pl.BlockSpec(memory_space=pl.ANY)
LANES = 128
GROUP = 2


def in_hbm(value):
    return pltpu.with_memory_space_constraint(value, pltpu.HBM)


def mm(a, b):
    return jnp.dot(a, b, preferred_element_type=F32)


def mm_t(a, b):
    return lax.dot_general(a, b, (((1,), (1,)), ((), ())), preferred_element_type=F32)


def halves(value):
    high = value.astype(BF)
    return high, (value - high.astype(F32)).astype(BF)


def chained(steps):
    wholes = [steps[h] for h in range(steps.shape[0])]
    while len(wholes) > 1:
        joined = [
            jnp.dot(a, b, precision=HIGHEST, preferred_element_type=F32)
            for a, b in zip(wholes[::2], wholes[1::2])
        ]
        wholes = joined + wholes[2 * len(joined) :]
    return wholes[0]


def fetch_steps(up, steps, sems, col):
    depth = steps.shape[0]
    cols = 1 << depth
    copies = []
    for h in range(depth):
        node = 2 * cols - 2 * (cols >> h) + (col >> h)
        copies.append(pltpu.make_async_copy(up.at[0, node], steps.at[h], sems.at[h]))
    return copies


def one_hot(low, size):
    rows = lax.broadcasted_iota(jnp.int32, (size, low.shape[1]), 0).astype(BF)
    wanted = jnp.broadcast_to(low.astype(BF), rows.shape)
    return jnp.where(rows == wanted, jnp.ones_like(rows), jnp.zeros_like(rows))


def up_kernel(
    place, x_hbm, order_hbm, basis_hbm, leaf_up_hbm, up, lifted, first_out, second_out, poles, ordered,
    x, order, basis, leaf_up, steps, sems, step_sems,
):
    leaf_count, rank, points = basis.shape
    rhs = x.shape[0]
    half = leaf_count // 2
    edge = 2 * REACH
    col, cols = place[0], lifted.shape[0]
    first = [
        pltpu.make_async_copy(order_hbm, order, sems.at[0]),
        pltpu.make_async_copy(x_hbm, x, sems.at[1]),
    ]
    first += fetch_steps(up, steps, step_sems, col)
    second = [pltpu.make_async_copy(basis_hbm, basis, sems.at[2])]
    third = [pltpu.make_async_copy(leaf_up_hbm, leaf_up, sems.at[3])]
    for copy in first + second + third:
        copy.start()
    for copy in first:
        copy.wait()
    whole = chained(steps)
    slabs = jnp.concatenate(
        [x[:, a * points : (a + 1) * points] for a in range(leaf_count)], axis=0
    )
    leaves = []
    for i in range(leaf_count):
        where = order[:, i * points : (i + 1) * points]
        low = where & (points - 1)
        high = jnp.broadcast_to(where // points, (8, points))
        picked = mm(slabs, one_hot(low, points)).reshape(leaf_count, rhs // 8, 8, points)
        total = picked[0]
        for a in range(1, leaf_count):
            total = jnp.where((high == a)[None], picked[a], total)
        leaf = total.reshape(rhs, points).astype(BF)
        ordered[2 * i] = leaf[:, :LANES]
        ordered[2 * i + 1] = leaf[:, LANES:]
        leaves.append(leaf)
    for copy in second:
        copy.wait()
    group = points // rank
    lane = lax.broadcasted_iota(jnp.int32, (rhs, points), 1) // rank
    quads = []
    for i in range(0, leaf_count, group):
        crossed = mm_t(
            jnp.concatenate(leaves[i : i + group], axis=0),
            basis[i : i + group].reshape(group * rank, points),
        )
        quad = crossed[:rhs]
        for j in range(1, group):
            quad = jnp.where(lane == j, crossed[j * rhs : (j + 1) * rhs], quad)
        quads.append(quad.astype(BF))
    every = jnp.concatenate(quads, axis=1)
    pairs = [every[:, q * LANES : (q + 1) * LANES] for q in range(half)]
    for q in range(half):
        poles[q] = pairs[q]
        first_out[edge + q] = pairs[q]
        second_out[edge + q] = pairs[q]
    for copy in third:
        copy.wait()
    up_high, up_low = halves(leaf_up[...].reshape(leaf_count * rank, rank))
    top = mm(every, up_high) + mm(every, up_low)
    top = jnp.dot(top, whole, precision=HIGHEST, preferred_element_type=F32)
    packed = jnp.concatenate([top[: rhs // 2], top[rhs // 2 :]], axis=1)
    for c in range(cols):
        lifted[c] = packed
    odd = (col & 1) == 1
    head, tail = ordered[:edge], ordered[2 * leaf_count - edge :]
    first_out[:edge] = jnp.where(odd, tail, head)
    second_out[:edge] = jnp.where(odd, head, tail)


def up_call(place, inputs, order, basis, leaf_up, up_transfer, cols):
    rhs = inputs.shape[0]
    leaf_count, rank, points = basis.shape
    depth = cols.bit_length() - 1
    shape = jax.ShapeDtypeStruct
    half = leaf_count // 2
    sent = shape((2 * REACH + half, rhs, LANES), BF)
    return pl.pallas_call(
        up_kernel,
        out_shape=(
            shape((cols, rhs // 2, LANES), F32),
            sent,
            sent,
            shape((half, rhs, LANES), BF),
            shape((2 * leaf_count, rhs, LANES), BF),
        ),
        in_specs=[SMEM] + [ANY] * 5,
        out_specs=(VMEM,) * 5,
        scratch_shapes=[
            pltpu.VMEM(inputs.shape, BF),
            pltpu.VMEM(order.shape, order.dtype),
            pltpu.VMEM(basis.shape, BF),
            pltpu.VMEM(leaf_up.shape, F32),
            pltpu.VMEM((depth, rank, rank), F32),
            pltpu.SemaphoreType.DMA((4,)),
            pltpu.SemaphoreType.DMA((depth,)),
        ],
        compiler_params=pltpu.CompilerParams(vmem_limit_bytes=24 << 20),
        cost_estimate=pl.CostEstimate(flops=1 << 32, bytes_accessed=3 << 20, transcendentals=0),
        name="up",
    )(place, in_hbm(inputs), in_hbm(order), in_hbm(basis), in_hbm(leaf_up), in_hbm(up_transfer))


def near_kernel(
    place, offsets, ordered, first, second, blocks_hbm, up, near, extended, blocks, steps, sems, step_sems
):
    leaf_count, count, points, _ = blocks.shape
    col, row, rows, cols = place[0], place[1], place[2], place[3]
    edge = 2 * REACH
    group = leaf_count // sems.shape[0]
    fetched = [
        pltpu.make_async_copy(
            blocks_hbm.at[i : i + group], blocks.at[i : i + group], sems.at[i // group]
        )
        for i in range(0, leaf_count, group)
    ]
    small = fetch_steps(up, steps, step_sems, col)
    for copy in small + fetched:
        copy.start()
    odd = (col & 1) == 1
    lowest = (col == 0) & (row == 0)
    highest = (col == cols - 1) & (row == rows - 1)
    before = jnp.where(odd, second[:edge], first[:edge])
    after = jnp.where(odd, first[:edge], second[:edge])
    extended[edge : edge + 2 * leaf_count] = ordered[...]
    extended[:edge] = jnp.where(lowest, jnp.zeros_like(before), before)
    extended[edge + 2 * leaf_count :] = jnp.where(highest, jnp.zeros_like(after), after)
    for i in range(leaf_count):
        if i % group == 0:
            fetched[i // group].wait()
        if i == leaf_count - 2:
            for copy in small:
                copy.wait()
            whole = chained(steps)
            half = whole.shape[0] // 2
            near[leaf_count, :half, : 2 * half] = whole[:half]
            near[leaf_count, :half, LANES : LANES + 2 * half] = whole[half:]
        parts = []
        for k in range(count):
            at = 2 * (i + REACH + offsets[k, i])
            parts += [extended[at], extended[at + 1]]
        near[i] = mm(jnp.concatenate(parts, axis=1), blocks[i].reshape(count * points, points))


def near_call(place, offsets, ordered, first, second, near_blocks, up_transfer, cols):
    leaf_count, _, points, _ = near_blocks.shape
    rank = up_transfer.shape[-1]
    depth = cols.bit_length() - 1
    rhs = ordered.shape[1]
    return pl.pallas_call(
        near_kernel,
        out_shape=jax.ShapeDtypeStruct((leaf_count + 1, rhs, points), F32),
        in_specs=[SMEM, SMEM] + [VMEM] * 3 + [ANY] * 2,
        out_specs=VMEM,
        scratch_shapes=[
            pltpu.VMEM((2 * leaf_count + 4 * REACH, rhs, LANES), BF),
            pltpu.VMEM(near_blocks.shape, BF),
            pltpu.VMEM((depth, rank, rank), F32),
            pltpu.SemaphoreType.DMA((leaf_count // GROUP,)),
            pltpu.SemaphoreType.DMA((depth,)),
        ],
        compiler_params=pltpu.CompilerParams(vmem_limit_bytes=24 << 20),
        cost_estimate=pl.CostEstimate(flops=1 << 30, bytes_accessed=1 << 20, transcendentals=0),
        name="near",
    )(place, offsets, ordered, first, second, in_hbm(near_blocks), in_hbm(up_transfer))


def down_kernel(
    place, lists, row_lists, first, second, around, p1, p3, couple, rows, couple_row, leaf_up,
    basis, near, order, out, poles, spread, marks,
):
    leaf_count, rank, points = basis.shape
    rhs = near.shape[1]
    slots = couple.shape[1]
    edge = 2 * REACH
    col, cols = place[0], place[3]
    odd = (col & 1) == 1
    poles[0] = jnp.where(col == 0, around[...], jnp.where(odd, second[edge:], first[edge:]))
    poles[1] = p1[...]
    poles[2] = jnp.where(col == cols - 1, around[...], jnp.where(odd, first[edge:], second[edge:]))
    poles[3] = p3[...]

    for i in range(leaf_count):
        where = order[:, i * points : (i + 1) * points]
        marks[:, i * points : (i + 1) * points] = one_hot(where & (points - 1), points)
    joined = []
    for i in range(leaf_count):
        parts = []
        for k in range(slots):
            source = lists[k, i] & (leaf_count - 1)
            pair = poles[k, source // 2]
            parts.append(jnp.where((source & 1) == 1, pair[:, rank:], pair[:, :rank]))
        joined.append(jnp.concatenate(parts, axis=1))
    sources = []
    for k in range(couple_row.shape[1]):
        packed = rows[row_lists[0, k]]
        sources.append(jnp.concatenate([packed[:, :rank], packed[:, rank:]], axis=0))
    local_row = mm(
        jnp.concatenate(sources, axis=1), couple_row[0].reshape(len(sources) * rank, rank)
    )
    sides = [mm(joined[i], couple[i].reshape(slots * rank, rank)) for i in range(leaf_count)]
    half = rank // 2
    whole = jnp.concatenate(
        [near[leaf_count, :half, :rank], near[leaf_count, :half, LANES : LANES + rank]], axis=0
    )
    downward = lax.dot_general(
        local_row, whole, (((1,), (1,)), ((), ())), precision=HIGHEST, preferred_element_type=F32
    )
    down_high, down_low = halves(downward)
    up_high, up_low = halves(leaf_up[...].reshape(leaf_count * rank, rank))
    both = mm_t(jnp.concatenate([down_high, down_low], axis=0), up_high)
    pushed = both[:rhs] + both[rhs:] + mm_t(down_high, up_low)
    leaf_local = (jnp.concatenate(sides, axis=1) + pushed).astype(BF)
    group = points // rank
    lane = lax.broadcasted_iota(jnp.int32, (rhs, points), 1) // rank
    fars = []
    for i in range(0, leaf_count, group):
        several = leaf_local[:, i * rank : (i + group) * rank]
        apart = jnp.concatenate(
            [jnp.where(lane == j, several, jnp.zeros_like(several)) for j in range(group)], axis=0
        )
        together = mm(apart, basis[i : i + group].reshape(group * rank, points))
        fars += [together[j * rhs : (j + 1) * rhs] for j in range(group)]
    for i in range(leaf_count):
        high = (order[:, i * points : (i + 1) * points] // points).astype(BF)
        high = jnp.broadcast_to(high, (rhs, points))
        summed = (near[i] + fars[i]).astype(BF)
        for a in range(leaf_count):
            spread[a * rhs : (a + 1) * rhs, i * points : (i + 1) * points] = jnp.where(
                high == a, summed, jnp.zeros_like(summed)
            )
    total = mm_t(spread[...], marks[...]).astype(BF)
    for a in range(leaf_count):
        out[:, a * points : (a + 1) * points] = total[a * rhs : (a + 1) * rhs]


def down_call(
    place, lists, row_lists, first, second, around, p1, p3, couple, row_poles, couple_row, leaf_up,
    basis, near, order,
):
    leaf_count, rank, points = basis.shape
    rhs = near.shape[1]
    return pl.pallas_call(
        down_kernel,
        out_shape=jax.ShapeDtypeStruct((rhs, leaf_count * points), BF),
        in_specs=[SMEM] * 3 + [VMEM] * 12,
        out_specs=VMEM,
        scratch_shapes=[
            pltpu.VMEM((couple.shape[1], *p1.shape), BF),
            pltpu.VMEM((leaf_count * rhs, leaf_count * points), BF),
            pltpu.VMEM((points, leaf_count * points), BF),
        ],
        compiler_params=pltpu.CompilerParams(vmem_limit_bytes=24 << 20),
        cost_estimate=pl.CostEstimate(flops=1 << 28, bytes_accessed=3 << 20, transcendentals=0),
        name="down",
    )(
        place, lists, row_lists, first, second, around, p1, p3, couple, row_poles, couple_row,
        leaf_up, basis, near, order,
    )


def local(
    inputs,
    morton_order,
    basis,
    leaf_up,
    up_transfer,
    couple_leaf,
    leaf_lists,
    couple_row,
    row_lists,
    near_blocks,
    near_offsets,
):
    cols = lax.axis_size("col")
    rows = lax.axis_size("row")
    count = rows * cols
    place = jnp.stack([lax.axis_index("col"), lax.axis_index("row"), rows, cols]).astype(jnp.int32)
    order = morton_order.reshape(1, -1)
    lifted, first, second, poles, ordered = up_call(
        place, inputs, order, basis, leaf_up, up_transfer, cols
    )
    everyone = lax.all_to_all(lifted, "col", 0, 0, tiled=True)

    def swap(value, start):
        pairs = [(b, (b + 1) % count) for b in range(start, count, 2)]
        return lax.ppermute(value, ("row", "col"), pairs + [(b, a) for a, b in pairs])

    def from_peer(value, away):
        return lax.ppermute(value, "col", [((c + away) % cols, c) for c in range(cols)])

    first = swap(first, 1)
    row_wire = everyone.sum(axis=0).astype(BF)
    row_wire = jnp.broadcast_to(row_wire[None], (rows,) + row_wire.shape)
    row_poles = lax.all_to_all(row_wire, "row", 0, 0, tiled=True)
    second = swap(second, 0)
    p1 = from_peer(poles, cols // 2)
    p3 = from_peer(poles, 2)
    down_rows = [(((r + 1) % rows) * cols + c, r * cols + c) for r in range(rows) for c in range(cols // 2)]
    up_rows = [(r * cols + c, ((r + 1) % rows) * cols + c) for r in range(rows) for c in range(cols // 2, cols)]
    turn = down_rows + up_rows
    around = lax.ppermute(first[2 * REACH :], ("row", "col"), turn)
    near = near_call(
        place, near_offsets.T, ordered, first, second, near_blocks, up_transfer, cols
    )
    return down_call(
        place, leaf_lists.T, row_lists, first, second, around, p1, p3, couple_leaf, row_poles, couple_row,
        leaf_up, basis, near, order,
    )


def solution(mesh):
    return jax.shard_map(
        local,
        mesh=mesh,
        in_specs=(
            P(None, ("row", "col")),
            P(("row", "col")),
            P(("row", "col"), None, None),
            P(),
            P("row", None, None, None),
            P(("row", "col"), None, None, None),
            P(("row", "col"), None),
            P("row", None, None, None),
            P("row", None),
            P(("row", "col"), None, None, None),
            P(("row", "col"), None),
        ),
        out_specs=P(None, ("row", "col")),
        check_vma=False,
    )
```

```python
import jax
import jax.numpy as jnp
from jax import lax
from jax.experimental import pallas as pl
from jax.experimental.pallas import tpu as pltpu
from jax.sharding import PartitionSpec as P

REACH = 4
BF = jnp.bfloat16
F32 = jnp.float32
HIGHEST = lax.Precision.HIGHEST
VMEM = pl.BlockSpec(memory_space=pltpu.VMEM)
SMEM = pl.BlockSpec(memory_space=pltpu.SMEM)
ANY = pl.BlockSpec(memory_space=pl.ANY)
LANES = 128
GROUP = 2


def in_hbm(value):
    return pltpu.with_memory_space_constraint(value, pltpu.HBM)


def mm(a, b):
    return jnp.dot(a, b, preferred_element_type=F32)


def mm_t(a, b):
    return lax.dot_general(a, b, (((1,), (1,)), ((), ())), preferred_element_type=F32)


def halves(value):
    high = value.astype(BF)
    return high, (value - high.astype(F32)).astype(BF)


def chained(steps):
    wholes = [steps[h] for h in range(steps.shape[0])]
    while len(wholes) > 1:
        joined = [
            jnp.dot(a, b, precision=HIGHEST, preferred_element_type=F32)
            for a, b in zip(wholes[::2], wholes[1::2])
        ]
        wholes = joined + wholes[2 * len(joined) :]
    return wholes[0]


def fetch_steps(up, steps, sems, col):
    depth = steps.shape[0]
    cols = 1 << depth
    copies = []
    for h in range(depth):
        node = 2 * cols - 2 * (cols >> h) + (col >> h)
        copies.append(pltpu.make_async_copy(up.at[0, node], steps.at[h], sems.at[h]))
    return copies


def one_hot(low, size):
    rows = lax.broadcasted_iota(jnp.int32, (size, low.shape[1]), 0).astype(BF)
    wanted = jnp.broadcast_to(low.astype(BF), rows.shape)
    return jnp.where(rows == wanted, jnp.ones_like(rows), jnp.zeros_like(rows))


def up_kernel(
    place, x_hbm, order_hbm, basis_hbm, leaf_up_hbm, up, lifted, first_out, second_out, poles, ordered,
    x, order, basis, leaf_up, steps, sems, step_sems,
):
    leaf_count, rank, points = basis.shape
    rhs = x.shape[0]
    half = leaf_count // 2
    edge = 2 * REACH
    col, cols = place[0], lifted.shape[0]
    first = [
        pltpu.make_async_copy(order_hbm, order, sems.at[0]),
        pltpu.make_async_copy(x_hbm, x, sems.at[1]),
    ]
    first += fetch_steps(up, steps, step_sems, col)
    second = [pltpu.make_async_copy(basis_hbm, basis, sems.at[2])]
    third = [pltpu.make_async_copy(leaf_up_hbm, leaf_up, sems.at[3])]
    for copy in first + second + third:
        copy.start()
    for copy in first:
        copy.wait()
    whole = chained(steps)
    slabs = jnp.concatenate(
        [x[:, a * points : (a + 1) * points] for a in range(leaf_count)], axis=0
    )
    leaves = []
    for i in range(leaf_count):
        where = order[:, i * points : (i + 1) * points]
        low = where & (points - 1)
        high = jnp.broadcast_to(where // points, (8, points))
        picked = mm(slabs, one_hot(low, points)).reshape(leaf_count, rhs // 8, 8, points)
        total = picked[0]
        for a in range(1, leaf_count):
            total = jnp.where((high == a)[None], picked[a], total)
        leaf = total.reshape(rhs, points).astype(BF)
        ordered[2 * i] = leaf[:, :LANES]
        ordered[2 * i + 1] = leaf[:, LANES:]
        leaves.append(leaf)
    for copy in second:
        copy.wait()
    group = points // rank
    lane = lax.broadcasted_iota(jnp.int32, (rhs, points), 1) // rank
    quads = []
    for i in range(0, leaf_count, group):
        crossed = mm_t(
            jnp.concatenate(leaves[i : i + group], axis=0),
            basis[i : i + group].reshape(group * rank, points),
        )
        quad = crossed[:rhs]
        for j in range(1, group):
            quad = jnp.where(lane == j, crossed[j * rhs : (j + 1) * rhs], quad)
        quads.append(quad.astype(BF))
    every = jnp.concatenate(quads, axis=1)
    pairs = [every[:, q * LANES : (q + 1) * LANES] for q in range(half)]
    for q in range(half):
        poles[q] = pairs[q]
        first_out[edge + q] = pairs[q]
        second_out[edge + q] = pairs[q]
    for copy in third:
        copy.wait()
    up_high, up_low = halves(leaf_up[...].reshape(leaf_count * rank, rank))
    top = mm(every, up_high) + mm(every, up_low)
    top = jnp.dot(top, whole, precision=HIGHEST, preferred_element_type=F32)
    packed = jnp.concatenate([top[: rhs // 2], top[rhs // 2 :]], axis=1)
    for c in range(cols):
        lifted[c] = packed
    odd = (col & 1) == 1
    head, tail = ordered[:edge], ordered[2 * leaf_count - edge :]
    first_out[:edge] = jnp.where(odd, tail, head)
    second_out[:edge] = jnp.where(odd, head, tail)


def up_call(place, inputs, order, basis, leaf_up, up_transfer, cols):
    rhs = inputs.shape[0]
    leaf_count, rank, points = basis.shape
    depth = cols.bit_length() - 1
    shape = jax.ShapeDtypeStruct
    half = leaf_count // 2
    sent = shape((2 * REACH + half, rhs, LANES), BF)
    return pl.pallas_call(
        up_kernel,
        out_shape=(
            shape((cols, rhs // 2, LANES), F32),
            sent,
            sent,
            shape((half, rhs, LANES), BF),
            shape((2 * leaf_count, rhs, LANES), BF),
        ),
        in_specs=[SMEM] + [ANY] * 5,
        out_specs=(VMEM,) * 5,
        scratch_shapes=[
            pltpu.VMEM(inputs.shape, BF),
            pltpu.VMEM(order.shape, order.dtype),
            pltpu.VMEM(basis.shape, BF),
            pltpu.VMEM(leaf_up.shape, F32),
            pltpu.VMEM((depth, rank, rank), F32),
            pltpu.SemaphoreType.DMA((4,)),
            pltpu.SemaphoreType.DMA((depth,)),
        ],
        compiler_params=pltpu.CompilerParams(vmem_limit_bytes=24 << 20),
        cost_estimate=pl.CostEstimate(flops=1 << 32, bytes_accessed=3 << 20, transcendentals=0),
        name="up",
    )(place, in_hbm(inputs), in_hbm(order), in_hbm(basis), in_hbm(leaf_up), in_hbm(up_transfer))


def ends_kernel(place, ends):
    lowest = (place[0] == 0) & (place[1] == 0)
    highest = (place[0] == place[3] - 1) & (place[1] == place[2] - 1)
    one = jnp.ones(ends.shape[1:], BF)
    ends[0] = jnp.where(lowest, jnp.zeros_like(one), one)
    ends[1] = jnp.where(highest, jnp.zeros_like(one), one)


def ends_call(place, rhs):
    return pl.pallas_call(
        ends_kernel,
        out_shape=jax.ShapeDtypeStruct((2, rhs, LANES), BF),
        in_specs=[SMEM],
        out_specs=VMEM,
        cost_estimate=pl.CostEstimate(flops=1 << 31, bytes_accessed=1 << 14, transcendentals=0),
        name="ends",
    )(place)


def near_kernel(
    place, offsets, ends, ordered, first, second, blocks_hbm, up, near, extended, blocks, steps, sems, step_sems
):
    leaf_count, count, points, _ = blocks.shape
    col = place[0]
    edge = 2 * REACH
    group = leaf_count // sems.shape[0]
    fetched = [
        pltpu.make_async_copy(
            blocks_hbm.at[i : i + group], blocks.at[i : i + group], sems.at[i // group]
        )
        for i in range(0, leaf_count, group)
    ]
    small = fetch_steps(up, steps, step_sems, col)
    for copy in small + fetched:
        copy.start()
    odd = (col & 1) == 1
    before = jnp.where(odd, second[:edge], first[:edge])
    after = jnp.where(odd, first[:edge], second[:edge])
    extended[edge : edge + 2 * leaf_count] = ordered[...]
    extended[:edge] = before * ends[0]
    extended[edge + 2 * leaf_count :] = after * ends[1]
    for i in range(leaf_count):
        if i % group == 0:
            fetched[i // group].wait()
        if i == leaf_count - 2:
            for copy in small:
                copy.wait()
            whole = chained(steps)
            half = whole.shape[0] // 2
            near[leaf_count, :half, : 2 * half] = whole[:half]
            near[leaf_count, :half, LANES : LANES + 2 * half] = whole[half:]
        parts = []
        for k in range(count):
            at = 2 * (i + REACH + offsets[k, i])
            parts += [extended[at], extended[at + 1]]
        near[i] = mm(jnp.concatenate(parts, axis=1), blocks[i].reshape(count * points, points))


def near_call(place, offsets, ordered, first, second, near_blocks, up_transfer, cols):
    leaf_count, _, points, _ = near_blocks.shape
    rank = up_transfer.shape[-1]
    depth = cols.bit_length() - 1
    rhs = ordered.shape[1]
    return pl.pallas_call(
        near_kernel,
        out_shape=jax.ShapeDtypeStruct((leaf_count + 1, rhs, points), F32),
        in_specs=[SMEM, SMEM] + [VMEM] * 4 + [ANY] * 2,
        out_specs=VMEM,
        scratch_shapes=[
            pltpu.VMEM((2 * leaf_count + 4 * REACH, rhs, LANES), BF),
            pltpu.VMEM(near_blocks.shape, BF),
            pltpu.VMEM((depth, rank, rank), F32),
            pltpu.SemaphoreType.DMA((leaf_count // GROUP,)),
            pltpu.SemaphoreType.DMA((depth,)),
        ],
        compiler_params=pltpu.CompilerParams(vmem_limit_bytes=24 << 20),
        cost_estimate=pl.CostEstimate(flops=1 << 30, bytes_accessed=1 << 20, transcendentals=0),
        name="near",
    )(place, offsets, ends_call(place, rhs), ordered, first, second, in_hbm(near_blocks), in_hbm(up_transfer))


def down_kernel(
    place, lists, row_lists, first, second, around, p1, p3, couple, rows, couple_row, leaf_up,
    basis, near, order, out, poles, spread, marks,
):
    leaf_count, rank, points = basis.shape
    rhs = near.shape[1]
    slots = couple.shape[1]
    edge = 2 * REACH
    col, cols = place[0], place[3]
    odd = (col & 1) == 1
    poles[0] = jnp.where(col == 0, around[...], jnp.where(odd, second[edge:], first[edge:]))
    poles[1] = p1[...]
    poles[2] = jnp.where(col == cols - 1, around[...], jnp.where(odd, first[edge:], second[edge:]))
    poles[3] = p3[...]

    for i in range(leaf_count):
        where = order[:, i * points : (i + 1) * points]
        marks[:, i * points : (i + 1) * points] = one_hot(where & (points - 1), points)
    joined = []
    for i in range(leaf_count):
        parts = []
        for k in range(slots):
            source = lists[k, i] & (leaf_count - 1)
            pair = poles[k, source // 2]
            parts.append(jnp.where((source & 1) == 1, pair[:, rank:], pair[:, :rank]))
        joined.append(jnp.concatenate(parts, axis=1))
    sources = []
    for k in range(couple_row.shape[1]):
        packed = rows[row_lists[0, k]]
        sources.append(jnp.concatenate([packed[:, :rank], packed[:, rank:]], axis=0))
    local_row = mm(
        jnp.concatenate(sources, axis=1), couple_row[0].reshape(len(sources) * rank, rank)
    )
    sides = [mm(joined[i], couple[i].reshape(slots * rank, rank)) for i in range(leaf_count)]
    half = rank // 2
    whole = jnp.concatenate(
        [near[leaf_count, :half, :rank], near[leaf_count, :half, LANES : LANES + rank]], axis=0
    )
    downward = lax.dot_general(
        local_row, whole, (((1,), (1,)), ((), ())), precision=HIGHEST, preferred_element_type=F32
    )
    down_high, down_low = halves(downward)
    up_high, up_low = halves(leaf_up[...].reshape(leaf_count * rank, rank))
    both = mm_t(jnp.concatenate([down_high, down_low], axis=0), up_high)
    pushed = both[:rhs] + both[rhs:] + mm_t(down_high, up_low)
    leaf_local = (jnp.concatenate(sides, axis=1) + pushed).astype(BF)
    group = points // rank
    lane = lax.broadcasted_iota(jnp.int32, (rhs, points), 1) // rank
    fars = []
    for i in range(0, leaf_count, group):
        several = leaf_local[:, i * rank : (i + group) * rank]
        apart = jnp.concatenate(
            [jnp.where(lane == j, several, jnp.zeros_like(several)) for j in range(group)], axis=0
        )
        together = mm(apart, basis[i : i + group].reshape(group * rank, points))
        fars += [together[j * rhs : (j + 1) * rhs] for j in range(group)]
    for i in range(leaf_count):
        high = (order[:, i * points : (i + 1) * points] // points).astype(BF)
        high = jnp.broadcast_to(high, (rhs, points))
        summed = (near[i] + fars[i]).astype(BF)
        for a in range(leaf_count):
            spread[a * rhs : (a + 1) * rhs, i * points : (i + 1) * points] = jnp.where(
                high == a, summed, jnp.zeros_like(summed)
            )
    total = mm_t(spread[...], marks[...]).astype(BF)
    for a in range(leaf_count):
        out[:, a * points : (a + 1) * points] = total[a * rhs : (a + 1) * rhs]


def down_call(
    place, lists, row_lists, first, second, around, p1, p3, couple, row_poles, couple_row, leaf_up,
    basis, near, order,
):
    leaf_count, rank, points = basis.shape
    rhs = near.shape[1]
    return pl.pallas_call(
        down_kernel,
        out_shape=jax.ShapeDtypeStruct((rhs, leaf_count * points), BF),
        in_specs=[SMEM] * 3 + [VMEM] * 12,
        out_specs=VMEM,
        scratch_shapes=[
            pltpu.VMEM((couple.shape[1], *p1.shape), BF),
            pltpu.VMEM((leaf_count * rhs, leaf_count * points), BF),
            pltpu.VMEM((points, leaf_count * points), BF),
        ],
        compiler_params=pltpu.CompilerParams(vmem_limit_bytes=24 << 20),
        cost_estimate=pl.CostEstimate(flops=1 << 28, bytes_accessed=3 << 20, transcendentals=0),
        name="down",
    )(
        place, lists, row_lists, first, second, around, p1, p3, couple, row_poles, couple_row,
        leaf_up, basis, near, order,
    )


def local(
    inputs,
    morton_order,
    basis,
    leaf_up,
    up_transfer,
    couple_leaf,
    leaf_lists,
    couple_row,
    row_lists,
    near_blocks,
    near_offsets,
):
    cols = lax.axis_size("col")
    rows = lax.axis_size("row")
    count = rows * cols
    place = jnp.stack([lax.axis_index("col"), lax.axis_index("row"), rows, cols]).astype(jnp.int32)
    order = morton_order.reshape(1, -1)
    lifted, first, second, poles, ordered = up_call(
        place, inputs, order, basis, leaf_up, up_transfer, cols
    )
    everyone = lax.all_to_all(lifted, "col", 0, 0, tiled=True)

    def swap(value, start):
        pairs = [(b, (b + 1) % count) for b in range(start, count, 2)]
        return lax.ppermute(value, ("row", "col"), pairs + [(b, a) for a, b in pairs])

    def from_peer(value, away):
        return lax.ppermute(value, "col", [((c + away) % cols, c) for c in range(cols)])

    first = swap(first, 1)
    row_wire = everyone.sum(axis=0).astype(BF)
    row_wire = jnp.broadcast_to(row_wire[None], (rows,) + row_wire.shape)
    row_poles = lax.all_to_all(row_wire, "row", 0, 0, tiled=True)
    second = swap(second, 0)
    p1 = from_peer(poles, cols // 2)
    p3 = from_peer(poles, 2)
    down_rows = [(((r + 1) % rows) * cols + c, r * cols + c) for r in range(rows) for c in range(cols // 2)]
    up_rows = [(r * cols + c, ((r + 1) % rows) * cols + c) for r in range(rows) for c in range(cols // 2, cols)]
    turn = down_rows + up_rows
    around = lax.ppermute(first[2 * REACH :], ("row", "col"), turn)
    near = near_call(
        place, near_offsets.T, ordered, first, second, near_blocks, up_transfer, cols
    )
    return down_call(
        place, leaf_lists.T, row_lists, first, second, around, p1, p3, couple_leaf, row_poles, couple_row,
        leaf_up, basis, near, order,
    )


def solution(mesh):
    return jax.shard_map(
        local,
        mesh=mesh,
        in_specs=(
            P(None, ("row", "col")),
            P(("row", "col")),
            P(("row", "col"), None, None),
            P(),
            P("row", None, None, None),
            P(("row", "col"), None, None, None),
            P(("row", "col"), None),
            P("row", None, None, None),
            P("row", None),
            P(("row", "col"), None, None, None),
            P(("row", "col"), None),
        ),
        out_specs=P(None, ("row", "col")),
        check_vma=False,
    )
```
